32 devices in a mesh: cd: 8 (over z, y), ab: 4 (over x, core).
Axes of the slice: x: 2, y: 2, z: 4, core: 2. Of those that a mesh axis runs over, the one named last changes fastest.
Arguments:
- amplitudes: bfloat16 [512, 8, 800], P('cd', None, 'ab'), may hold values from -6 to 6
- integrals: bfloat16 [8, 800, 2048], P('cd', None, 'ab'), may hold values from -0.078125 to 0.078125
Outputs:
- ladder: float32 [512, 2048], P('cd', 'ab')
The draws below stay inside these ranges and needn't reach their ends.
All inputs are finite; a program needn't handle non-finite values.
Results may differ from the reference program's by a relative error of at most 0.0003.
Values may be sent and summed in bfloat16 or wider, within the bound.
A program may use at most 64 MiB of HBM per device.

```python
import jax
import jax.numpy as jnp

NPAIR = 512
DV = 800
CV = 8
AB = 2048


def steps_of(key, dims, shards, least, top_value):
    def one(dim, shards_of):
        draws = jax.random.uniform(jax.random.fold_in(jax.random.fold_in(key, 6), dim), (shards_of,), jnp.float32, least / len(shards), top_value / len(shards))
        return jnp.repeat(jnp.exp(draws), dims[dim] // shards_of).reshape((-1,) + (1,) * (len(dims) - dim - 1))

    gain = one(*shards[0])
    for cut in shards[1:]:
        gain = gain * one(*cut)
    return gain


def gaussian(key, extent, deviation, most, pieces=(), held_as=jnp.bfloat16):
    drawn = deviation * jax.random.normal(key, extent, jnp.float32)
    if pieces:
        drawn = drawn * steps_of(key, extent, pieces, -0.22, 0.18)
    return jnp.clip(drawn, -most, most).astype(held_as)


def setup_inputs(seed: int = 0) -> dict:
    key_of = jax.random.split(jax.random.key(seed), 3)
    return {
        "amplitudes": gaussian(key_of[0], (NPAIR, CV, DV), 1.0, 6.0, ((0, 8), (2, 4))),
        "integrals": gaussian(key_of[1], (CV, DV, AB), (CV * DV) ** -0.5, 0.078125, ((0, 8), (2, 4))),
    }


def reference(amplitudes, integrals):
    pairs = amplitudes.reshape(amplitudes.shape[0], amplitudes.shape[1] * amplitudes.shape[2])
    slab = integrals.reshape(integrals.shape[0] * integrals.shape[1], integrals.shape[2])
    return jnp.dot(pairs, slab, preferred_element_type=jnp.float32)
```

```python
import functools

import jax
import jax.numpy as jnp
from jax import lax
from jax.experimental import pallas as pl
from jax.experimental.pallas import tpu as pltpu
from jax.sharding import PartitionSpec as P

MESH = pl.DeviceIdType.MESH
LANES = 128
ORDER = (7, 5, 6, 3, 4, 1, 2, 0)


def flip(index, bits):
    out = index
    bit = 1
    while bit <= bits:
        if bits & bit:
            out = out + bit - 2 * bit * (lax.div(index, bit) % 2)
        bit *= 2
    return out


def kernel(
    amp_ref, int_ref, out_ref, stage, held, slab, ysend, yrecv, zsum, zrecv,
    a2a_s, a2a_r, xf_s, xf_r, cf_s, cf_r, y_s, y_r, z_s, z_r, local_sem,
):
    cd = lax.axis_index("cd")
    ab = lax.axis_index("ab")
    rows, n_cd, width = amp_ref.shape
    wide = stage.shape[2]
    n_ab = slab.shape[0]
    columns = int_ref.shape[1]
    half = n_cd // 2

    peers = [(flip(cd, k), ab) for k in range(1, n_cd)]
    peers += [(cd, flip(ab, 1)), (cd, flip(ab, 2))]
    barrier = pltpu.get_barrier_semaphore()
    for peer in peers:
        pl.semaphore_signal(barrier, inc=1, device_id=peer, device_id_type=MESH)

    stage[:, :, width:] = jnp.zeros((n_cd, rows, wide - width), stage.dtype)
    for c in range(n_cd):
        stage[c, :, :width] = amp_ref[:, c, :]

    pl.semaphore_wait(barrier, len(peers))

    def remote(src, dst, s, r, peer):
        return pltpu.make_async_remote_copy(
            src_ref=src, dst_ref=dst, send_sem=s, recv_sem=r,
            device_id=peer, device_id_type=MESH,
        )

    a2a = {}
    for k in ORDER:
        if k:
            a2a[k] = remote(stage.at[flip(cd, k)], held.at[0, k], a2a_s.at[k], a2a_r.at[k], (flip(cd, k), ab))
            a2a[k].start()
    own = pltpu.make_async_copy(stage.at[cd], held.at[0, 0], local_sem)
    own.start()

    for j in range(n_ab):
        slab[j, :width, :] = int_ref[j * width : (j + 1) * width, :]
        slab[j, width:, :] = jnp.zeros((wide - width, columns), slab.dtype)

    xf = {k: remote(held.at[0, k], held.at[2, k], xf_s.at[k], xf_r.at[k], (cd, flip(ab, 2))) for k in ORDER}
    cf = {
        (r, k): remote(held.at[r, k], held.at[r + 1, k], cf_s.at[r // 2, k], cf_r.at[r // 2, k], (cd, flip(ab, 1)))
        for k in ORDER
        for r in (0, 2)
    }
    ycopy = {
        h: remote(ysend.at[h], yrecv.at[h], y_s.at[h], y_r.at[h], (flip(cd, 1), ab)) for h in range(half)
    }
    zcopy = {
        h: remote(zsum.at[h], zrecv.at[h], z_s.at[h], z_r.at[h], (flip(cd, 2 * h), ab)) for h in range(1, half)
    }

    def arrive(k):
        (a2a[k].wait_recv if k else own.wait)()
        xf[k].start()
        cf[0, k].start()

    def relay(k):
        xf[k].wait_recv()
        cf[2, k].start()

    def product(k):
        cf[0, k].wait_recv()
        cf[2, k].wait_recv()
        total = jnp.dot(held[0, k], slab[ab], preferred_element_type=jnp.float32)
        for r in range(1, n_ab):
            total += jnp.dot(held[r, k], slab[flip(ab, r)], preferred_element_type=jnp.float32)
        if k % 2:
            ysend[k // 2] = total
            ycopy[k // 2].start()
        else:
            zsum[k // 2] = total

    def collect(h):
        ycopy[h].wait_recv()
        zsum[h] += yrecv[h]
        if h:
            zcopy[h].start()

    after = {6: 3, 4: 2}
    for step, k in enumerate(ORDER):
        arrive(k)
        if step >= 1:
            relay(ORDER[step - 1])
        if step >= 2:
            product(ORDER[step - 2])
        if step >= 3 and ORDER[step - 3] in after:
            collect(after[ORDER[step - 3]])
    relay(ORDER[-1])
    product(ORDER[-2])
    collect(1)
    product(ORDER[-1])
    collect(0)
    total = zsum[0]
    for h in range(half - 1, 0, -1):
        zcopy[h].wait_recv()
        total += zrecv[h]
    out_ref[...] = total

    for k in ORDER:
        if k:
            a2a[k].wait_send()
        xf[k].wait_send()
        cf[0, k].wait_send()
        cf[2, k].wait_send()
    for h in range(half):
        ycopy[h].wait_send()
        if h:
            zcopy[h].wait_send()


def by_kernel(amplitudes, integrals, n_ab):
    rows, n_cd, width = amplitudes.shape
    columns = integrals.shape[2]
    wide = -(-width // LANES) * LANES
    half = n_cd // 2
    dma = pltpu.SemaphoreType.DMA
    block = pltpu.VMEM((half, rows, columns), jnp.float32)
    return pl.pallas_call(
        kernel,
        out_shape=jax.ShapeDtypeStruct((rows, columns), jnp.float32),
        in_specs=[pl.BlockSpec(memory_space=pltpu.VMEM)] * 2,
        out_specs=pl.BlockSpec(memory_space=pltpu.VMEM),
        scratch_shapes=[
            pltpu.VMEM((n_cd, rows, wide), amplitudes.dtype),
            pltpu.VMEM((n_ab, n_cd, rows, wide), amplitudes.dtype),
            pltpu.VMEM((n_ab, wide, columns), integrals.dtype),
            block, block, block, block,
            dma((n_cd,)), dma((n_cd,)), dma((n_cd,)), dma((n_cd,)),
            dma((2, n_cd)), dma((2, n_cd)),
            dma((half,)), dma((half,)), dma((half,)), dma((half,)),
            dma,
        ],
        compiler_params=pltpu.CompilerParams(
            collective_id=0, has_side_effects=True, vmem_limit_bytes=32 * 1024 * 1024
        ),
    )(amplitudes, integrals.reshape(integrals.shape[1], columns))


def by_collectives(amplitudes, integrals):
    c_local, depth, columns = integrals.shape
    mine = lax.all_to_all(amplitudes, "cd", split_axis=1, concat_axis=0, tiled=True)
    complete = lax.all_gather(mine, "ab", axis=2, tiled=True)
    flat = complete.reshape(complete.shape[0], c_local * depth)
    slab = integrals.reshape(c_local * depth, columns)
    partial = jnp.dot(flat, slab, preferred_element_type=jnp.float32)
    return lax.psum_scatter(partial, "cd", scatter_dimension=0, tiled=True)


def on_device(n_cd, n_ab, amplitudes, integrals):
    rows = amplitudes.shape[0]
    if n_cd == 8 and n_ab == 4 and integrals.shape[0] == 1 and rows % 16 == 0:
        return by_kernel(amplitudes, integrals, n_ab)
    return by_collectives(amplitudes, integrals)


def solution(mesh):
    specs = (P("cd", None, "ab"), P("cd", None, "ab"))
    return jax.shard_map(
        functools.partial(on_device, mesh.shape["cd"], mesh.shape["ab"]),
        mesh=mesh, in_specs=specs, out_specs=P("cd", "ab"), check_vma=False,
    )
```

```python
import functools

import jax
import jax.numpy as jnp
from jax import lax
from jax.experimental import pallas as pl
from jax.experimental.pallas import tpu as pltpu
from jax.sharding import PartitionSpec as P

MESH = pl.DeviceIdType.MESH
LANES = 128
ORDER = (5, 7, 3, 1, 4, 6, 2, 0)
DIRECT = ()
PLAN = (
    ("a", 5), ("r", 5), ("a", 7), ("p", 5), ("a", 3), ("a", 1), ("r", 7), ("p", 7),
    ("a", 4), ("a", 6), ("a", 2), ("r", 3), ("p", 3), ("r", 1), ("p", 1),
    ("r", 4), ("p", 4), ("s", 2), ("r", 6), ("p", 6), ("s", 3),
    ("r", 2), ("p", 2), ("s", 1), ("r", 0), ("p", 0), ("s", 0),
)


def flip(index, bits):
    out = index
    bit = 1
    while bit <= bits:
        if bits & bit:
            out = out + bit - 2 * bit * (lax.div(index, bit) % 2)
        bit *= 2
    return out


def kernel(
    amp_ref, int_ref, out_ref, stage, held, slab, ysend, yrecv, zsum, zrecv,
    amp, whole, a2a_s, a2a_r, xf_s, xf_r, cf_s, cf_r, y_s, y_r, z_s, z_r, local_sem,
):
    cd = lax.axis_index("cd")
    ab = lax.axis_index("ab")
    rows, n_cd, width = amp_ref.shape
    wide = stage.shape[2]
    n_ab = slab.shape[0]
    columns = int_ref.shape[1]
    half = n_cd // 2

    load_amp = pltpu.make_async_copy(amp_ref, amp, local_sem.at[0])
    load_int = pltpu.make_async_copy(int_ref, whole, local_sem.at[1])
    load_amp.start()
    load_int.start()
    peers = [(flip(cd, k), ab) for k in range(1, n_cd)]
    peers += [(cd, flip(ab, 1)), (cd, flip(ab, 2))]
    peers += [(flip(cd, k), flip(ab, 2)) for k in DIRECT]
    barrier = pltpu.get_barrier_semaphore()
    for peer in peers:
        pl.semaphore_signal(barrier, inc=1, device_id=peer, device_id_type=MESH)

    stage[:, :, width:] = jnp.zeros((n_cd, rows, wide - width), stage.dtype)
    load_amp.wait()
    for c in range(n_cd):
        stage[c, :, :width] = amp[:, c, :]

    pl.semaphore_wait(barrier, len(peers))

    def remote(src, dst, s, r, peer):
        return pltpu.make_async_remote_copy(
            src_ref=src, dst_ref=dst, send_sem=s, recv_sem=r,
            device_id=peer, device_id_type=MESH,
        )

    def block(r, k):
        return held.at[r, k] if r or k else stage.at[cd]

    a2a, xf = {}, {}
    for k in ORDER:
        away = flip(cd, k)
        if k:
            a2a[k] = remote(stage.at[away], held.at[0, k], a2a_s.at[k], a2a_r.at[k], (away, ab))
            a2a[k].start()
        if k in DIRECT:
            xf[k] = remote(stage.at[away], held.at[2, k], xf_s.at[k], xf_r.at[k], (away, flip(ab, 2)))
            xf[k].start()
        else:
            xf[k] = remote(block(0, k), held.at[2, k], xf_s.at[k], xf_r.at[k], (cd, flip(ab, 2)))
    cf = {
        (r, k): remote(block(r, k), held.at[r + 1, k], cf_s.at[r // 2, k], cf_r.at[r // 2, k], (cd, flip(ab, 1)))
        for k in ORDER
        for r in (0, 2)
    }
    xf[0].start()
    cf[0, 0].start()

    load_int.wait()
    for j in range(n_ab):
        slab[j, :width, :] = whole[j * width : (j + 1) * width, :]
        slab[j, width:, :] = jnp.zeros((wide - width, columns), slab.dtype)

    ycopy = {
        h: remote(ysend.at[h], yrecv.at[h], y_s.at[h], y_r.at[h], (flip(cd, 1), ab)) for h in range(half)
    }
    zcopy = {
        h: remote(zsum.at[h], zrecv.at[h], z_s.at[h], z_r.at[h], (flip(cd, 2 * h), ab)) for h in range(1, half)
    }

    def arrive(k):
        a2a[k].wait_recv()
        if k not in DIRECT:
            xf[k].start()
        cf[0, k].start()

    def relay(k):
        xf[k].wait_recv()
        cf[2, k].start()

    def product(k):
        cf[0, k].wait_recv()
        cf[2, k].wait_recv()
        total = jnp.dot(block(0, k)[...], slab[ab], preferred_element_type=jnp.float32)
        for r in range(1, n_ab):
            total += jnp.dot(held[r, k], slab[flip(ab, r)], preferred_element_type=jnp.float32)
        if k % 2:
            ysend[k // 2] = total
            ycopy[k // 2].start()
        else:
            zsum[k // 2] = total

    def collect(h):
        ycopy[h].wait_recv()
        zsum[h] += yrecv[h]
        if h:
            zcopy[h].start()

    act = {"a": arrive, "r": relay, "p": product, "s": collect}
    for what, k in PLAN:
        act[what](k)
    total = zsum[0]
    for h in (2, 3, 1):
        zcopy[h].wait_recv()
        total += zrecv[h]
    out_ref[...] = total

    for k in ORDER:
        if k:
            a2a[k].wait_send()
        xf[k].wait_send()
        cf[0, k].wait_send()
        cf[2, k].wait_send()
    for h in range(half):
        ycopy[h].wait_send()
        if h:
            zcopy[h].wait_send()


def by_kernel(amplitudes, integrals, n_ab):
    rows, n_cd, width = amplitudes.shape
    columns = integrals.shape[2]
    wide = -(-width // LANES) * LANES
    half = n_cd // 2
    dma = pltpu.SemaphoreType.DMA
    block = pltpu.VMEM((half, rows, columns), jnp.float32)
    return pl.pallas_call(
        kernel,
        out_shape=jax.ShapeDtypeStruct((rows, columns), jnp.float32),
        in_specs=[pl.BlockSpec(memory_space=pltpu.HBM)] * 2,
        out_specs=pl.BlockSpec(memory_space=pltpu.VMEM),
        scratch_shapes=[
            pltpu.VMEM((n_cd, rows, wide), amplitudes.dtype),
            pltpu.VMEM((n_ab, n_cd, rows, wide), amplitudes.dtype),
            pltpu.VMEM((n_ab, wide, columns), integrals.dtype),
            block, block, block, block,
            pltpu.VMEM(amplitudes.shape, amplitudes.dtype),
            pltpu.VMEM(integrals.shape[1:], integrals.dtype),
            dma((n_cd,)), dma((n_cd,)), dma((n_cd,)), dma((n_cd,)),
            dma((2, n_cd)), dma((2, n_cd)),
            dma((half,)), dma((half,)), dma((half,)), dma((half,)),
            dma((2,)),
        ],
        compiler_params=pltpu.CompilerParams(
            collective_id=0, has_side_effects=True, vmem_limit_bytes=56 * 1024 * 1024
        ),
    )(amplitudes, integrals.reshape(integrals.shape[1], columns))


def by_collectives(amplitudes, integrals):
    c_local, depth, columns = integrals.shape
    mine = lax.all_to_all(amplitudes, "cd", split_axis=1, concat_axis=0, tiled=True)
    complete = lax.all_gather(mine, "ab", axis=2, tiled=True)
    flat = complete.reshape(complete.shape[0], c_local * depth)
    slab = integrals.reshape(c_local * depth, columns)
    partial = jnp.dot(flat, slab, preferred_element_type=jnp.float32)
    return lax.psum_scatter(partial, "cd", scatter_dimension=0, tiled=True)


def on_device(n_cd, n_ab, amplitudes, integrals):
    rows = amplitudes.shape[0]
    if n_cd == 8 and n_ab == 4 and integrals.shape[0] == 1 and rows % 16 == 0:
        return by_kernel(amplitudes, integrals, n_ab)
    return by_collectives(amplitudes, integrals)


def solution(mesh):
    specs = (P("cd", None, "ab"), P("cd", None, "ab"))
    return jax.shard_map(
        functools.partial(on_device, mesh.shape["cd"], mesh.shape["ab"]),
        mesh=mesh, in_specs=specs, out_specs=P("cd", "ab"), check_vma=False,
    )
```
